32 devices in a mesh: dp: 8 (over z, x), row: 2 (over y), col: 2 (over core).
Axes of the slice: x: 2, y: 2, z: 4, core: 2. Of those that a mesh axis runs over, the one named last changes fastest.
Arguments:
- tokens: bfloat16 [2048, 1024], P(('dp', 'row'), 'col'), may hold values from -40 to 40
- cotangent: bfloat16 [2048, 1024], P(('dp', 'row'), 'col'), may hold values from -6 to 6
- w_query: bfloat16 [1024, 2048], P('col', 'row'), may hold values from -0.1875 to 0.1875
- key_weight: bfloat16 [1024, 1024], P('col', 'row'), may hold values from -0.1875 to 0.1875
- value_weight: bfloat16 [1024, 1024], P('col', 'row'), may hold values from -0.1875 to 0.1875
- w_output: bfloat16 [2048, 1024], P('row', 'col'), may hold values from -1 to 1
- w_gate: bfloat16 [1024, 3072], P('col', 'row'), may hold values from -0.1875 to 0.1875
- w_up: bfloat16 [1024, 3072], P('col', 'row'), may hold values from -0.1875 to 0.1875
- w_down: bfloat16 [3072, 1024], P('row', 'col'), may hold values from -0.109375 to 0.109375
- gain_attn: float32 [1024], P('col'), may hold values from 0.5 to 1.5
- gain_query: float32 [128], replicated, may hold values from 0.5 to 1.5
- gain_key: float32 [128], replicated, may hold values from 0.5 to 1.5
- gain_mlp: float32 [1024], P('col'), may hold values from 0.5 to 1.5
- seq_lengths: int32 [24], replicated, may hold values from 1 to 254, as said below
- seq_groups: int32 [24], replicated, may hold values from 0 to 7, as said below
Outputs:
- mixed: bfloat16 [2048, 1024], P(('dp', 'row'), 'col')
- input_grad: float32 [2048, 1024], P(('dp', 'row'), 'col')
- w_query_grad: float32 [1024, 2048], P(('col', 'dp'), 'row')
- w_key_grad: float32 [1024, 1024], P(('col', 'dp'), 'row')
- w_value_grad: float32 [1024, 1024], P(('col', 'dp'), 'row')
- w_output_grad: float32 [2048, 1024], P(('row', 'dp'), 'col')
- w_gate_grad: float32 [1024, 3072], P(('col', 'dp'), 'row')
- w_up_grad: float32 [1024, 3072], P(('col', 'dp'), 'row')
- w_down_grad: float32 [3072, 1024], P(('row', 'dp'), 'col')
- gain_attn_grad: float32 [1024], P('col')
- gain_query_grad: float32 [128], replicated
- gain_key_grad: float32 [128], replicated
- gain_mlp_grad: float32 [1024], P('col')
The draws below stay inside these ranges and needn't reach their ends.
Inputs may be any that keep to these rules, and one draw needn't show every extreme that they name: `seq_lengths`: the 3 sequences that seq_groups gives to one index of dp fill its 256 rows from the first, one after another in the order of their numbers, and total at most 256; one of them is longer than 128; in some index they total exactly 256. `seq_groups`: every index of dp holds exactly 3 sequences.
All inputs are finite; a program needn't handle non-finite values.
Results may differ from the reference program's by a relative error of at most 0.012.
Values may be sent and summed in bfloat16 or wider, within the bound.
A program may use at most 128 MiB of HBM per device.

```python
import math
import jax
import jax.numpy as jnp
from jax import lax

MODEL_WIDTH = 1024
QUERY_HEAD_COUNT = 16
VALUE_HEADS = 8
HEAD_SIZE = 128
FF = 3072
TG = 256
SEQ_GROUP = 3
TOKENS = 2048
NSEQ = 24


def split_layout(key):
    first, second, third, fourth, fifth = jax.random.split(key, 5)
    groups_count = NSEQ // SEQ_GROUP
    order = jax.random.permutation(first, NSEQ).astype(jnp.int32)
    group = (order // SEQ_GROUP).astype(jnp.int32)
    member = order % SEQ_GROUP
    longest = jax.random.randint(third, (groups_count,), 0, SEQ_GROUP)
    filled = jax.random.randint(fourth, (), 0, groups_count)
    is_long = member == longest[group]
    short = jax.random.randint(second, (NSEQ,), 1, TG // 8 + 1)
    short = jnp.where(group == filled, 1, short)
    others = jax.ops.segment_sum(jnp.where(is_long, 0, short), group, num_segments=groups_count)
    upper = TG - others[group]
    lower = TG // 2 + 1
    spread = jax.random.randint(fifth, (NSEQ,), 0, 1 << 20)
    long_len = lower + spread % (upper - lower + 1)
    long_len = jnp.where(group == filled, upper, long_len)
    lengths = jnp.where(is_long, long_len, short).astype(jnp.int32)
    return (lengths, group)


def draw_seq_lengths(key, part):
    lengths, group = split_layout(key)
    return lengths


def draw_seq_groups(key, part):
    lengths, group = split_layout(key)
    return group


def draw_tokens(key, part):
    key = jax.random.fold_in(key, 7)
    first, second = jax.random.split(key, 2)
    column = jnp.exp(jax.random.uniform(second, (1, MODEL_WIDTH), jnp.float32, 0.0, math.log(10.0))) * 0.25
    base = jnp.clip(jax.random.normal(first, (TOKENS, MODEL_WIDTH), jnp.float32), -4.0, 4.0)
    return (base * column).astype(jnp.bfloat16)


def levels(key, shape, pieces, low, top_value):
    def one(dim, shards_of):
        steps = jax.random.uniform(jax.random.fold_in(jax.random.fold_in(key, 6), dim), (shards_of,), jnp.float32, low / len(pieces), top_value / len(pieces))
        return jnp.repeat(jnp.exp(steps), shape[dim] // shards_of).reshape((-1,) + (1,) * (len(shape) - dim - 1))

    loudness = one(*pieces[0])
    for cut in pieces[1:]:
        loudness = loudness * one(*cut)
    return loudness


def gaussian(stream_key, dims, deviation, limit, shards=(), kind=jnp.bfloat16):
    values = deviation * jax.random.normal(stream_key, dims, jnp.float32)
    if shards:
        values = values * levels(stream_key, dims, shards, -0.22, 0.18)
    return jnp.clip(values, -limit, limit).astype(kind)


def setup_inputs(seed: int = 0) -> dict:
    streams_of = jax.random.split(jax.random.key(seed), 16)
    tokens = draw_tokens(jax.random.fold_in(streams_of[15], 71), 0)
    cotangent = gaussian(streams_of[1], (TOKENS, MODEL_WIDTH), 1.0, 6.0, ((0, 16), (1, 2)))
    w_query = gaussian(streams_of[2], (MODEL_WIDTH, QUERY_HEAD_COUNT * HEAD_SIZE), MODEL_WIDTH ** -0.5, 0.1875, ((0, 2), (1, 2)))
    key_weight = gaussian(streams_of[3], (MODEL_WIDTH, VALUE_HEADS * HEAD_SIZE), MODEL_WIDTH ** -0.5, 0.1875, ((0, 2), (1, 2)))
    value_weight = gaussian(streams_of[4], (MODEL_WIDTH, VALUE_HEADS * HEAD_SIZE), MODEL_WIDTH ** -0.5, 0.1875, ((0, 2), (1, 2)))
    w_output = gaussian(streams_of[5], (QUERY_HEAD_COUNT * HEAD_SIZE, MODEL_WIDTH), (QUERY_HEAD_COUNT * HEAD_SIZE * 4 // TG) ** -0.5, 1.0, ((0, 2), (1, 2)))
    w_gate = gaussian(streams_of[6], (MODEL_WIDTH, FF), MODEL_WIDTH ** -0.5, 0.1875, ((0, 2), (1, 2)))
    w_up = gaussian(streams_of[7], (MODEL_WIDTH, FF), MODEL_WIDTH ** -0.5, 0.1875, ((0, 2), (1, 2)))
    w_down = gaussian(streams_of[8], (FF, MODEL_WIDTH), FF ** -0.5, 0.109375, ((0, 2), (1, 2)))
    gain_attn = jnp.clip(1.0 + 0.1 * jax.random.normal(streams_of[9], (MODEL_WIDTH,), jnp.float32), 0.5, 1.5)
    gain_query = jnp.clip(1.0 + 0.1 * jax.random.normal(streams_of[10], (HEAD_SIZE,), jnp.float32), 0.5, 1.5)
    gain_key = jnp.clip(1.0 + 0.1 * jax.random.normal(streams_of[11], (HEAD_SIZE,), jnp.float32), 0.5, 1.5)
    gain_mlp = jnp.clip(1.0 + 0.1 * jax.random.normal(streams_of[12], (MODEL_WIDTH,), jnp.float32), 0.5, 1.5)
    seq_lengths = draw_seq_lengths(jax.random.fold_in(streams_of[15], 71), 0)
    seq_groups = draw_seq_groups(jax.random.fold_in(streams_of[15], 71), 0)
    return {"tokens": tokens, "cotangent": cotangent, "w_query": w_query, "key_weight": key_weight, "value_weight": value_weight, "w_output": w_output, "w_gate": w_gate, "w_up": w_up, "w_down": w_down, "gain_attn": gain_attn, "gain_query": gain_query, "gain_key": gain_key, "gain_mlp": gain_mlp, "seq_lengths": seq_lengths, "seq_groups": seq_groups}


EPS = 1e-06
THETA = 1000000.0
NEGATIVE = -1e+30

@jax.custom_vjp
def reduced_precision(v):
    return lax.optimization_barrier(v.astype(jnp.bfloat16)).astype(jnp.float32)

@jax.custom_vjp
def reduced_backward(v):
    return v

def low_keep(v):
    return (reduced_precision(v), None)

def low_pass(kept, grad):
    return (grad,)

def back_keep(v):
    return (v, None)

def back_low(kept, grad):
    return (reduced_precision(grad),)
reduced_precision.defvjp(low_keep, low_pass)
reduced_backward.defvjp(back_keep, back_low)

def layout(lengths, groups, group, slots):
    count = lengths.shape[0]
    mine = groups == group
    sizes_here = jnp.where(mine, lengths, 0).astype(jnp.int32)
    starts = (jnp.cumsum(sizes_here) - sizes_here).astype(jnp.int32)
    place = lax.broadcasted_iota(jnp.int32, (slots, count), 0)
    number = lax.broadcasted_iota(jnp.int32, (slots, count), 1)
    inside = mine[None, :] & (place >= starts[None, :]) & (place < (starts + sizes_here)[None, :])
    found = lax.optimization_barrier(jnp.sum(inside.astype(jnp.int32), axis=1)).astype(jnp.int32)
    segment = lax.optimization_barrier(jnp.sum(jnp.where(inside, number, 0), axis=1)).astype(jnp.int32)
    spot = lax.broadcasted_iota(jnp.int32, (slots,), 0)
    segment = jnp.where(found > 0, segment, count + spot).astype(jnp.int32)
    position = lax.optimization_barrier(jnp.sum(jnp.where(inside, place - starts[None, :], 0), axis=1)).astype(jnp.int32)
    return (segment, position)

def allowed_pairs(segment):
    slots = segment.shape[0]
    later = lax.broadcasted_iota(jnp.int32, (slots, slots), 0)
    earlier = lax.broadcasted_iota(jnp.int32, (slots, slots), 1)
    return (segment[:, None] == segment[None, :]) & (earlier <= later)

def rotate(value_rows, position):
    size = value_rows.shape[-1]
    half = size // 2
    freq = THETA ** (-(jnp.arange(half, dtype=jnp.float32) * 2.0 / size))
    angle = position.astype(jnp.float32)[:, None] * freq[None, :]
    cosine = jnp.cos(angle)[:, None, :]
    sine = jnp.sin(angle)[:, None, :]
    first = value_rows[..., :half]
    second = value_rows[..., half:]
    return jnp.concatenate([first * cosine - second * sine, second * cosine + first * sine], axis=-1)

def rms_scale(value_rows, gain):
    return value_rows * lax.rsqrt(lax.optimization_barrier(jnp.mean(value_rows * value_rows, axis=-1, keepdims=True)) + EPS) * gain

def dense_matrix(left, right):
    return jnp.dot(left, right, precision=lax.Precision.HIGHEST)

def group_layer(inputs, w_query, key_weight, value_weight, w_output, w_gate, w_up, w_down, gain_attn, gain_query, gain_key, gain_mlp, segment, position):
    token_rows = inputs.shape[0]
    normed_rows = reduced_precision(rms_scale(inputs, gain_attn))
    query = reduced_backward(dense_matrix(normed_rows, w_query)).reshape(token_rows, QUERY_HEAD_COUNT, HEAD_SIZE)
    key_rows = reduced_backward(dense_matrix(normed_rows, key_weight)).reshape(token_rows, VALUE_HEADS, HEAD_SIZE)
    value_rows = reduced_precision(reduced_backward(dense_matrix(normed_rows, value_weight))).reshape(token_rows, VALUE_HEADS, HEAD_SIZE)
    query = reduced_precision(rotate(rms_scale(query, gain_query), position))
    key_rows = reduced_precision(rotate(rms_scale(key_rows, gain_key), position))
    rank_share = QUERY_HEAD_COUNT // VALUE_HEADS
    key_rows = jnp.repeat(key_rows, rank_share, axis=1)
    value_rows = jnp.repeat(value_rows, rank_share, axis=1)
    scores = jnp.einsum('qhd,khd->hqk', query, key_rows, precision=lax.Precision.HIGHEST)
    scores = reduced_backward(scores * (1.0 / math.sqrt(HEAD_SIZE)))
    scores = jnp.where(allowed_pairs(segment)[None], scores, NEGATIVE)
    probs = jax.nn.softmax(scores, axis=-1)
    attended = jnp.einsum('hqk,khd->qhd', reduced_precision(probs), value_rows, precision=lax.Precision.HIGHEST)
    attended = reduced_precision(reduced_backward(attended)).reshape(token_rows, QUERY_HEAD_COUNT * HEAD_SIZE)
    hidden = inputs + reduced_backward(dense_matrix(attended, w_output))
    normed_mlp = reduced_precision(rms_scale(hidden, gain_mlp))
    gate = reduced_backward(dense_matrix(normed_mlp, w_gate))
    up_part = reduced_backward(dense_matrix(normed_mlp, w_up))
    activated = reduced_precision(jax.nn.silu(gate) * up_part)
    return hidden + reduced_backward(dense_matrix(activated, w_down))

def reference(tokens, cotangent, w_query, key_weight, value_weight, w_output, w_gate, w_up, w_down, gain_attn, gain_query, gain_key, gain_mlp, seq_lengths, seq_groups):
    count = tokens.shape[0] // TG
    inputs = tokens.astype(jnp.float32).reshape(count, TG, MODEL_WIDTH)
    grads_out = cotangent.astype(jnp.float32).reshape(count, TG, MODEL_WIDTH)
    params = (w_query.astype(jnp.float32), key_weight.astype(jnp.float32), value_weight.astype(jnp.float32), w_output.astype(jnp.float32), w_gate.astype(jnp.float32), w_up.astype(jnp.float32), w_down.astype(jnp.float32), gain_attn.astype(jnp.float32), gain_query.astype(jnp.float32), gain_key.astype(jnp.float32), gain_mlp.astype(jnp.float32))

    def one_group(totals, item):
        rows_in, rows_grad, index = item
        segment, position = layout(seq_lengths, seq_groups, index, TG)

        def forward(inner, *weights):
            return group_layer(inner, *weights, segment, position)
        result, pull = jax.vjp(forward, rows_in, *params)
        grads = pull(rows_grad)
        totals = tuple((total + grad for total, grad in zip(totals, grads[1:])))
        return (totals, (result, grads[0]))
    zeros = tuple((jnp.zeros_like(param) for param in params))
    totals, (results, input_grads) = lax.scan(one_group, zeros, (inputs, grads_out, jnp.arange(count, dtype=jnp.int32)))
    mixed = results.reshape(count * TG, MODEL_WIDTH).astype(jnp.bfloat16)
    input_grad = input_grads.reshape(count * TG, MODEL_WIDTH)
    return (mixed, input_grad, totals[0], totals[1], totals[2], totals[3], totals[4], totals[5], totals[6], totals[7], totals[8], totals[9], totals[10])
```

```python
import math

import jax
import jax.numpy as jnp
from jax import lax
from jax.sharding import PartitionSpec as P

EPS = 1e-06
THETA = 1000000.0
NEGATIVE = -1e30


def layout(lengths, groups, group, slots):
    count = lengths.shape[0]
    mine = groups == group
    sizes_here = jnp.where(mine, lengths, 0)
    starts = jnp.cumsum(sizes_here) - sizes_here
    place = lax.broadcasted_iota(jnp.int32, (slots, count), 0)
    number = lax.broadcasted_iota(jnp.int32, (slots, count), 1)
    inside = mine[None, :] & (place >= starts[None, :]) & (place < (starts + sizes_here)[None, :])
    found = jnp.sum(inside.astype(jnp.int32), axis=1)
    segment = jnp.sum(jnp.where(inside, number, 0), axis=1)
    spot = lax.broadcasted_iota(jnp.int32, (slots,), 0)
    segment = jnp.where(found > 0, segment, count + spot)
    position = jnp.sum(jnp.where(inside, place - starts[None, :], 0), axis=1)
    return (segment, position)


def rotate(value_rows, position):
    size = value_rows.shape[-1]
    half = size // 2
    freq = THETA ** (-(jnp.arange(half, dtype=jnp.float32) * 2.0 / size))
    angle = position.astype(jnp.float32)[:, None] * freq[None, :]
    cosine = jnp.cos(angle)[:, None, :]
    sine = jnp.sin(angle)[:, None, :]
    first = value_rows[..., :half]
    second = value_rows[..., half:]
    return jnp.concatenate(
        [first * cosine - second * sine, second * cosine + first * sine], axis=-1
    )


def rms_scale(value_rows, gain):
    return (
        value_rows
        * lax.rsqrt(jnp.mean(value_rows * value_rows, axis=-1, keepdims=True) + EPS)
        * gain
    )


def swiglu(gate, up_part):
    return jax.nn.silu(gate) * up_part


def product(left, right):
    return jnp.dot(left, right, preferred_element_type=jnp.float32)


def contract_rows(left, right):
    return lax.dot_general(
        left, right, (((0,), (0,)), ((), ())), preferred_element_type=jnp.float32
    )


def contract_cols(left, right):
    return lax.dot_general(
        left, right, (((1,), (1,)), ((), ())), preferred_element_type=jnp.float32
    )


def attend(query_low, key_low, value_low, allowed, scale):
    token_rows, key_heads, head_dim = key_low.shape
    rank_share = query_low.shape[1] // key_heads
    grouped = query_low.reshape(token_rows, key_heads, rank_share, head_dim)
    raw = jnp.einsum("qhgd,khd->hgqk", grouped, key_low, preferred_element_type=jnp.float32)
    scores = jnp.where(allowed, raw * scale, NEGATIVE)
    top = jnp.max(scores, axis=-1, keepdims=True)
    exponent = jnp.exp(scores - top)
    total = jnp.sum(exponent, axis=-1, keepdims=True)
    probs = exponent / total
    attended = jnp.einsum(
        "hgqk,khd->qhgd", probs.astype(jnp.bfloat16), value_low, preferred_element_type=jnp.float32
    )
    return (attended.reshape(token_rows, key_heads * rank_share, head_dim), probs)


def attend_back(query_low, key_low, value_low, attended_grad, probs, scale):
    token_rows, key_heads, head_dim = key_low.shape
    rank_share = query_low.shape[1] // key_heads
    grouped = query_low.reshape(token_rows, key_heads, rank_share, head_dim)
    grad_grouped = attended_grad.reshape(token_rows, key_heads, rank_share, head_dim)
    prob_grad = jnp.einsum(
        "qhgd,khd->hgqk", grad_grouped, value_low, preferred_element_type=jnp.float32
    )
    inner = jnp.sum(probs * prob_grad, axis=-1, keepdims=True)
    score_grad = (probs * (prob_grad - inner)).astype(jnp.bfloat16)
    query_grad = (
        jnp.einsum("hgqk,khd->qhgd", score_grad, key_low, preferred_element_type=jnp.float32)
        * scale
    )
    key_grad = (
        jnp.einsum("hgqk,qhgd->khd", score_grad, grouped, preferred_element_type=jnp.float32)
        * scale
    )
    value_grad = jnp.einsum(
        "hgqk,qhgd->khd",
        probs.astype(jnp.bfloat16),
        grad_grouped,
        preferred_element_type=jnp.float32,
    )
    return (
        query_grad.reshape(token_rows, key_heads * rank_share, head_dim),
        key_grad,
        value_grad.astype(jnp.bfloat16),
    )


def swap(value, axis):
    return lax.ppermute(value, axis, [(0, 1), (1, 0)])


def flip(value, axis, bit):
    size = lax.axis_size(axis)
    return lax.ppermute(value, axis, [(i, i ^ bit) for i in range(size)])


def relative_order(size):
    bits = size.bit_length() - 1
    return [int(format(k, "b").zfill(bits)[::-1], 2) if bits else 0 for k in range(size)]


def relative_blocks(value_rows, axis):
    size = lax.axis_size(axis)
    me = lax.axis_index(axis)
    width = value_rows.shape[1] // size
    turned = value_rows.T.reshape(size, width, value_rows.shape[0])
    parts = [
        lax.dynamic_index_in_dim(turned, me ^ j, 0, keepdims=False) for j in relative_order(size)
    ]
    return jnp.concatenate(parts, axis=0)


def scattered_product(left, right, axis):
    size = lax.axis_size(axis)
    blocks = relative_blocks(left, axis)
    half = blocks.shape[0] // 2
    away = product(blocks[half:], right).astype(jnp.bfloat16)
    arrived = flip(away, axis, 1)
    kept = product(blocks[:half], right) + arrived.astype(jnp.float32)
    bit = 2
    while bit < size:
        half = kept.shape[0] // 2
        arrived = flip(kept[half:].astype(jnp.bfloat16), axis, bit)
        kept = kept[:half] + arrived.astype(jnp.float32)
        bit *= 2
    return kept


def total_over(value, axis):
    size = lax.axis_size(axis)
    bit = 1
    while bit < size:
        value = value + flip(value, axis, bit)
        bit *= 2
    return value


def pick(value, index, dim):
    half = value.shape[dim] // 2
    return lax.dynamic_slice_in_dim(value, index * half, half, dim)


def shards(
    tokens,
    cotangent,
    w_query,
    key_weight,
    value_weight,
    w_output,
    w_gate,
    w_up,
    w_down,
    gain_attn,
    gain_query,
    gain_key,
    gain_mlp,
    seq_lengths,
    seq_groups,
):
    half_rows, columns = tokens.shape
    width = columns * 2
    group_rows = half_rows * 2
    head_dim = gain_query.shape[0]
    scale = 1.0 / math.sqrt(head_dim)
    row = lax.axis_index("row")
    col = lax.axis_index("col")
    mine, theirs = col, 1 - col
    low = jnp.bfloat16

    def exchange_tokens(local):
        own = jnp.concatenate([local, swap(local, "row")], axis=0)
        return own, swap(own, "col")

    x_own_low, x_other_low = exchange_tokens(tokens)
    gains_own = jnp.stack([gain_attn, gain_mlp])
    gains_other = swap(gains_own, "col")
    qkv_keep = jnp.concatenate(
        [pick(w_query, mine, 1), pick(key_weight, mine, 1), pick(value_weight, mine, 1)], axis=1
    )
    qkv_other = swap(
        jnp.concatenate(
            [pick(w_query, theirs, 1), pick(key_weight, theirs, 1), pick(value_weight, theirs, 1)],
            axis=1,
        ),
        "col",
    )
    mlp_keep = jnp.concatenate([pick(w_gate, mine, 1), pick(w_up, mine, 1)], axis=1)
    mlp_theirs = jnp.concatenate([pick(w_gate, theirs, 1), pick(w_up, theirs, 1)], axis=1)
    mlp_other = swap(mlp_theirs, "col")
    output_mine, output_theirs = pick(w_output, mine, 0), pick(w_output, theirs, 0)
    output_other = swap(output_theirs, "col")
    down_mine, down_theirs = pick(w_down, mine, 0), pick(w_down, theirs, 0)
    down_other = swap(down_theirs, "col")
    cot_own, cot_other = exchange_tokens(cotangent)

    segment, position = layout(seq_lengths, seq_groups, lax.axis_index("dp"), group_rows)

    def own_first(vector):
        return jnp.where(row == 0, vector, jnp.roll(vector, half_rows))

    spot = own_first(lax.iota(jnp.int32, group_rows))
    segment, position = own_first(segment), own_first(position)
    allowed = (segment[:, None] == segment[None, :]) & (spot[None, :] <= spot[:, None])

    x_own = x_own_low.astype(jnp.float32)
    x_other = x_other_low.astype(jnp.float32)

    def inverse_of(own, other):
        total = jnp.sum(own * own, axis=1) + jnp.sum(other * other, axis=1)
        return lax.rsqrt(total / width + EPS)[:, None]

    inverse_attn = inverse_of(x_own, x_other)
    normed_own = (x_own * inverse_attn * gains_own[0]).astype(low)
    normed_other = (x_other * inverse_attn * gains_other[0]).astype(low)
    sums = product(normed_own, qkv_keep) + product(normed_other, qkv_other)
    query_wide = w_query.shape[1] // 2
    key_wide = key_weight.shape[1] // 2
    query_heads = query_wide // head_dim
    key_heads = key_wide // head_dim
    query_sum = sums[:, :query_wide]
    key_sum = sums[:, query_wide : query_wide + key_wide]
    value_sum = sums[:, query_wide + key_wide :]

    def turn(value_rows, gain):
        return rotate(rms_scale(value_rows, gain), position)

    query_rot, query_pull = jax.vjp(
        turn, query_sum.reshape(group_rows, query_heads, head_dim), gain_query
    )
    key_rot, key_pull = jax.vjp(turn, key_sum.reshape(group_rows, key_heads, head_dim), gain_key)
    query_low = query_rot.astype(low)
    key_low = key_rot.astype(low)
    value_low = value_sum.astype(low).reshape(group_rows, key_heads, head_dim)
    attended, probs = attend(query_low, key_low, value_low, allowed, scale)
    attended_own = attended.reshape(group_rows, query_wide).astype(low)
    attended_other = swap(attended_own, "col")
    partial_out = product(attended_own, output_mine) + product(attended_other, output_theirs)
    hidden = x_own + partial_out + swap(partial_out.astype(low), "row").astype(
        jnp.float32
    )[jnp.r_[half_rows:group_rows, 0:half_rows]]
    hidden_low_other = swap(hidden.astype(low), "col")
    hidden_other = hidden_low_other.astype(jnp.float32)
    inverse_mlp = inverse_of(hidden, hidden_other)
    mlp_own = (hidden * inverse_mlp * gains_own[1]).astype(low)
    mlp_rest = (hidden_other * inverse_mlp * gains_other[1]).astype(low)
    both = product(mlp_own, mlp_keep) + product(mlp_rest, mlp_other)
    units = both.shape[1] // 2
    gate, up_part = both[:, :units], both[:, units:]
    activated, swish_pull = jax.vjp(swiglu, gate, up_part)
    act_grad = contract_cols(cot_own, down_mine) + contract_cols(cot_other, down_other)
    gate_grad, up_grad = swish_pull(act_grad)
    grads_own = jnp.concatenate([gate_grad, up_grad], axis=1).astype(low)
    grads_other = swap(grads_own, "col")
    mlp_partial = contract_cols(grads_own, mlp_keep) + contract_cols(grads_other, mlp_theirs)
    normed_mlp_grad = mlp_partial + swap(mlp_partial.astype(low), "row").astype(
        jnp.float32
    )[jnp.r_[half_rows:group_rows, 0:half_rows]]
    grad_other = swap(normed_mlp_grad.astype(low), "col").astype(jnp.float32)
    scaled_own = normed_mlp_grad * gains_own[1]
    scaled_other = grad_other * gains_other[1]
    inner = (
        jnp.sum(scaled_own * hidden, axis=1) + jnp.sum(scaled_other * hidden_other, axis=1)
    )[:, None] / width
    cube = inverse_mlp**3 * inner
    hidden_grad = cot_own.astype(jnp.float32) + inverse_mlp * scaled_own - hidden * cube
    hidden_grad_other = (
        cot_other.astype(jnp.float32) + inverse_mlp * scaled_other - hidden_other * cube
    )
    gain_mlp_part = jnp.sum(
        (normed_mlp_grad * hidden * inverse_mlp)[:half_rows], axis=0
    )
    back_own = hidden_grad.astype(low)
    back_other = hidden_grad_other.astype(low)
    attended_grad = (
        contract_cols(back_own, output_mine) + contract_cols(back_other, output_other)
    ).astype(low)
    query_grad, key_grad, value_grad = attend_back(
        query_low,
        key_low,
        value_low,
        attended_grad.reshape(group_rows, query_heads, head_dim),
        probs,
        scale,
    )
    query_pre, gain_query_part = query_pull(query_grad)
    key_pre, gain_key_part = key_pull(key_grad)
    pre_own = jnp.concatenate(
        [
            query_pre.reshape(group_rows, query_wide).astype(low),
            key_pre.reshape(group_rows, key_wide).astype(low),
            value_grad.reshape(group_rows, key_wide),
        ],
        axis=1,
    )
    pre_other = swap(pre_own, "col")

    def whole(own, other, dim):
        first = jnp.where(col == 0, own, other)
        second = jnp.where(col == 0, other, own)
        return jnp.concatenate([first, second], axis=dim)

    qkv_theirs = jnp.concatenate(
        [pick(w_query, theirs, 1), pick(key_weight, theirs, 1), pick(value_weight, theirs, 1)],
        axis=1,
    )
    attn_partial = contract_cols(pre_own, qkv_keep) + contract_cols(pre_other, qkv_theirs)
    arrived = swap(attn_partial[half_rows:].astype(low), "row")
    normed_attn_grad = attn_partial[:half_rows] + arrived.astype(jnp.float32)
    x_mine = x_own[:half_rows]
    inverse_mine = inverse_attn[:half_rows]
    scaled = normed_attn_grad * gain_attn
    dot = jnp.sum(scaled * x_mine, axis=1).reshape(1, half_rows)
    dot = ((dot + swap(dot, "col")) / width).reshape(half_rows, 1)
    input_grad = (
        hidden_grad[:half_rows] + inverse_mine * scaled - x_mine * inverse_mine**3 * dot
    )
    gain_attn_part = jnp.sum(normed_attn_grad * x_mine * inverse_mine, axis=0)

    activated_own = activated.astype(low)
    activated_other = swap(activated_own, "col")
    down_partial = product(activated_own, down_mine) + product(activated_other, down_theirs)
    mixed = (
        hidden[:half_rows]
        + down_partial[:half_rows]
        + swap(down_partial[half_rows:].astype(low), "row").astype(jnp.float32)
    ).astype(low)

    down_total = scattered_product(whole(activated_own, activated_other, 1), cot_own, "dp")
    grads_first = jnp.where(col == 0, grads_own, grads_other)
    grads_second = jnp.where(col == 0, grads_other, grads_own)
    mlp_total = scattered_product(
        mlp_own,
        jnp.concatenate(
            [
                grads_first[:, :units],
                grads_second[:, :units],
                grads_first[:, units:],
                grads_second[:, units:],
            ],
            axis=1,
        ),
        "dp",
    )
    output_total = scattered_product(whole(attended_own, attended_other, 1), back_own, "dp")
    pre_first = jnp.where(col == 0, pre_own, pre_other)
    pre_second = jnp.where(col == 0, pre_other, pre_own)
    cuts = (0, query_wide, query_wide + key_wide, query_wide + 2 * key_wide)
    pre_whole = jnp.concatenate(
        [
            part[:, cuts[i] : cuts[i + 1]]
            for i in range(3)
            for part in (pre_first, pre_second)
        ],
        axis=1,
    )
    qkv_total = scattered_product(normed_own, pre_whole, "dp")
    edge = 2 * query_wide
    step = 2 * key_wide

    small = jnp.concatenate([gain_attn_part, gain_mlp_part, gain_query_part, gain_key_part])
    small = small.reshape(-1, 128)
    small = total_over(total_over(small, "dp"), "row").reshape(-1)
    heads_part = small[2 * columns :]
    heads_part = heads_part + swap(heads_part, "col")
    return (
        mixed,
        input_grad,
        qkv_total[:, :edge],
        qkv_total[:, edge : edge + step],
        qkv_total[:, edge + step :],
        output_total,
        mlp_total[:, : 2 * units],
        mlp_total[:, 2 * units :],
        down_total,
        small[:columns],
        heads_part[:head_dim],
        heads_part[head_dim:],
        small[columns : 2 * columns],
    )


def solution(mesh):
    in_specs = (
        P(("dp", "row"), "col"),
        P(("dp", "row"), "col"),
        P("col", "row"),
        P("col", "row"),
        P("col", "row"),
        P("row", "col"),
        P("col", "row"),
        P("col", "row"),
        P("row", "col"),
        P("col"),
        P(),
        P(),
        P("col"),
        P(),
        P(),
    )
    out_specs = (
        P(("dp", "row"), "col"),
        P(("dp", "row"), "col"),
        P(("col", "dp"), "row"),
        P(("col", "dp"), "row"),
        P(("col", "dp"), "row"),
        P(("row", "dp"), "col"),
        P(("col", "dp"), "row"),
        P(("col", "dp"), "row"),
        P(("row", "dp"), "col"),
        P("col"),
        P(),
        P(),
        P("col"),
    )
    return jax.shard_map(shards, mesh=mesh, in_specs=in_specs, out_specs=out_specs, check_vma=False)
```

```python
import functools
import math

import jax
import jax.numpy as jnp
from jax import lax
from jax.experimental import pallas as pl
from jax.experimental.pallas import tpu as pltpu
from jax.sharding import PartitionSpec as P

EPS = 1e-06
THETA = 1000000.0
NEGATIVE = -1e30


def layout(lengths, groups, group, slots):
    count = lengths.shape[0]
    mine = groups == group
    sizes_here = jnp.where(mine, lengths, 0)
    starts = jnp.cumsum(sizes_here) - sizes_here
    place = lax.broadcasted_iota(jnp.int32, (slots, count), 0)
    number = lax.broadcasted_iota(jnp.int32, (slots, count), 1)
    inside = mine[None, :] & (place >= starts[None, :]) & (place < (starts + sizes_here)[None, :])
    found = jnp.sum(inside.astype(jnp.int32), axis=1)
    segment = jnp.sum(jnp.where(inside, number, 0), axis=1)
    spot = lax.broadcasted_iota(jnp.int32, (slots,), 0)
    segment = jnp.where(found > 0, segment, count + spot)
    position = jnp.sum(jnp.where(inside, place - starts[None, :], 0), axis=1)
    return (segment, position)


def product(left, right):
    return jnp.dot(left, right, preferred_element_type=jnp.float32)


def contract_rows(left, right):
    return lax.dot_general(
        left, right, (((0,), (0,)), ((), ())), preferred_element_type=jnp.float32
    )


def contract_cols(left, right):
    return lax.dot_general(
        left, right, (((1,), (1,)), ((), ())), preferred_element_type=jnp.float32
    )


VMEM_BYTES = 44 * 1024 * 1024


def local_call(body, shapes, *operands):
    return pl.pallas_call(
        body,
        out_shape=[jax.ShapeDtypeStruct(shape, dtype) for shape, dtype in shapes],
        in_specs=[pl.BlockSpec(memory_space=pltpu.VMEM)] * len(operands),
        out_specs=[pl.BlockSpec(memory_space=pltpu.VMEM)] * len(shapes),
        compiler_params=pltpu.CompilerParams(vmem_limit_bytes=VMEM_BYTES),
    )(*operands)


def half_turn(value_rows):
    return pltpu.roll(value_rows, value_rows.shape[1] // 2, 1)


def head_scale(value_rows):
    return lax.rsqrt(jnp.mean(value_rows * value_rows, axis=1, keepdims=True) + EPS)


def head_cols(index, size):
    return slice(index * size, (index + 1) * size)


def softmax_rows(query, key, allowed, scale):
    scores = jnp.where(allowed, contract_cols(query, key) * scale, NEGATIVE)
    exponent = jnp.exp(scores - jnp.max(scores, axis=1, keepdims=True))
    return exponent / jnp.sum(exponent, axis=1, keepdims=True)


def attention_kernel(
    query_heads,
    key_heads,
    x_own_ref,
    x_other_ref,
    gain_own_ref,
    gain_other_ref,
    keep_ref,
    other_ref,
    gain_query_ref,
    gain_key_ref,
    cosine_ref,
    sine_ref,
    allowed_ref,
    normed_ref,
    inverse_ref,
    sums_ref,
    low_ref,
    attended_ref,
):
    size = gain_query_ref.shape[1]
    scale = 1.0 / math.sqrt(size)
    own = x_own_ref[...].astype(jnp.float32)
    other = x_other_ref[...].astype(jnp.float32)
    total = jnp.sum(own * own, axis=1, keepdims=True) + jnp.sum(
        other * other, axis=1, keepdims=True
    )
    inverse = lax.rsqrt(total / (2 * own.shape[1]) + EPS)
    inverse_ref[...] = inverse
    normed = (own * inverse * gain_own_ref[...]).astype(jnp.bfloat16)
    normed_ref[...] = normed
    normed_other = (other * inverse * gain_other_ref[...]).astype(jnp.bfloat16)
    sums_ref[...] = product(normed, keep_ref[...]) + product(normed_other, other_ref[...])
    cosine, sine = cosine_ref[...], sine_ref[...]
    for head in range(query_heads + key_heads):
        cols = head_cols(head, size)
        gain = gain_query_ref[...] if head < query_heads else gain_key_ref[...]
        one = sums_ref[:, cols]
        one = one * head_scale(one) * gain
        low_ref[:, cols] = (one * cosine + half_turn(one) * sine).astype(jnp.bfloat16)
    values = slice((query_heads + key_heads) * size, (query_heads + 2 * key_heads) * size)
    low_ref[:, values] = sums_ref[:, values].astype(jnp.bfloat16)
    allowed = allowed_ref[...] > 0.0
    share = query_heads // key_heads
    for head in range(query_heads):
        key = low_ref[:, head_cols(query_heads + head // share, size)]
        value = low_ref[:, head_cols(query_heads + key_heads + head // share, size)]
        cols = head_cols(head, size)
        probs = softmax_rows(low_ref[:, cols], key, allowed, scale)
        attended_ref[:, cols] = product(probs.astype(jnp.bfloat16), value).astype(jnp.bfloat16)


def attention_back_kernel(
    query_heads,
    key_heads,
    back_own_ref,
    back_other_ref,
    output_own_ref,
    output_other_ref,
    sums_ref,
    low_ref,
    gain_query_ref,
    gain_key_ref,
    cosine_ref,
    sine_ref,
    allowed_ref,
    pre_ref,
    gain_query_grad_ref,
    gain_key_grad_ref,
):
    size = gain_query_ref.shape[1]
    scale = 1.0 / math.sqrt(size)
    grad = (
        contract_cols(back_own_ref[...], output_own_ref[...])
        + contract_cols(back_other_ref[...], output_other_ref[...])
    ).astype(jnp.bfloat16)
    cosine, sine = cosine_ref[...], sine_ref[...]
    allowed = allowed_ref[...] > 0.0
    share = query_heads // key_heads

    def pull(rotated, head, gain):
        cols = head_cols(head, size)
        turned = rotated * cosine - half_turn(rotated) * sine
        one = sums_ref[:, cols]
        ratio = head_scale(one)
        weighted = turned * gain
        mean = jnp.mean(weighted * one, axis=1, keepdims=True)
        pre_ref[:, cols] = (ratio * weighted - one * ratio**3 * mean).astype(jnp.bfloat16)
        return jnp.sum(turned * one * ratio, axis=0, keepdims=True)

    gain_query_grad = jnp.zeros((1, size), jnp.float32)
    gain_key_grad = jnp.zeros((1, size), jnp.float32)
    for pair in range(key_heads):
        key = low_ref[:, head_cols(query_heads + pair, size)]
        value = low_ref[:, head_cols(query_heads + key_heads + pair, size)]
        key_rotated = jnp.zeros((key.shape[0], size), jnp.float32)
        value_grad = jnp.zeros((key.shape[0], size), jnp.float32)
        for head in range(pair * share, (pair + 1) * share):
            query = low_ref[:, head_cols(head, size)]
            grad_head = grad[:, head_cols(head, size)]
            probs = softmax_rows(query, key, allowed, scale)
            prob_grad = contract_cols(grad_head, value)
            inner = jnp.sum(probs * prob_grad, axis=1, keepdims=True)
            score_grad = (probs * (prob_grad - inner)).astype(jnp.bfloat16)
            gain_query_grad += pull(product(score_grad, key) * scale, head, gain_query_ref[...])
            key_rotated += contract_rows(score_grad, query)
            value_grad += contract_rows(probs.astype(jnp.bfloat16), grad_head)
        gain_key_grad += pull(key_rotated * scale, query_heads + pair, gain_key_ref[...])
        pre_ref[:, head_cols(query_heads + key_heads + pair, size)] = value_grad.astype(
            jnp.bfloat16
        )
    gain_query_grad_ref[...] = gain_query_grad
    gain_key_grad_ref[...] = gain_key_grad


def feed_forward_kernel(
    hidden_ref,
    other_ref,
    gain_own_ref,
    gain_other_ref,
    keep_ref,
    swapped_ref,
    act_grad_ref,
    normed_ref,
    inverse_ref,
    activated_ref,
    grads_ref,
):
    hidden = hidden_ref[...]
    other = other_ref[...].astype(jnp.float32)
    total = jnp.sum(hidden * hidden, axis=1, keepdims=True) + jnp.sum(
        other * other, axis=1, keepdims=True
    )
    inverse = lax.rsqrt(total / (2 * hidden.shape[1]) + EPS)
    inverse_ref[...] = inverse
    normed = (hidden * inverse * gain_own_ref[...]).astype(jnp.bfloat16)
    normed_ref[...] = normed
    normed_other = (other * inverse * gain_other_ref[...]).astype(jnp.bfloat16)
    units = activated_ref.shape[1]
    step = 256
    for start in range(0, units, step):
        low, high = slice(start, start + step), slice(units + start, units + start + step)
        gate = product(normed, keep_ref[:, low]) + product(normed_other, swapped_ref[:, low])
        up = product(normed, keep_ref[:, high]) + product(normed_other, swapped_ref[:, high])
        sigmoid = jax.nn.sigmoid(gate)
        silu = gate * sigmoid
        activated_ref[:, low] = (silu * up).astype(jnp.bfloat16)
        act_grad = act_grad_ref[:, low]
        grads_ref[:, low] = (act_grad * up * sigmoid * (1.0 + gate * (1.0 - sigmoid))).astype(
            jnp.bfloat16
        )
        grads_ref[:, high] = (act_grad * silu).astype(jnp.bfloat16)


def swap(value, axis):
    return lax.ppermute(value, axis, [(0, 1), (1, 0)])


def flip(value, axis, bit):
    size = lax.axis_size(axis)
    return lax.ppermute(value, axis, [(i, i ^ bit) for i in range(size)])


def relative_order(size):
    bits = size.bit_length() - 1
    return [int(format(k, "b").zfill(bits)[::-1], 2) if bits else 0 for k in range(size)]


def relative_blocks(value_rows, axis):
    size = lax.axis_size(axis)
    me = lax.axis_index(axis)
    width = value_rows.shape[1] // size
    turned = value_rows.T.reshape(size, width, value_rows.shape[0])
    parts = [
        lax.dynamic_index_in_dim(turned, me ^ j, 0, keepdims=False) for j in relative_order(size)
    ]
    return jnp.concatenate(parts, axis=0)


def first_half(left, axis):
    blocks = relative_blocks(left, axis)
    half = blocks.shape[0] // 2
    return blocks[:half], flip(blocks[half:], axis, 1)


def scattered_sum(kept, axis):
    bit = 2
    while bit < lax.axis_size(axis):
        half = kept.shape[0] // 2
        arrived = flip(kept[half:].astype(jnp.bfloat16), axis, bit)
        kept = kept[:half] + arrived.astype(jnp.float32)
        bit *= 2
    return kept


def pair_product(halves, right, right_arrived):
    return product(halves[0], right) + product(halves[1], right_arrived)


def total_over(value, axis):
    size = lax.axis_size(axis)
    bit = 1
    while bit < size:
        value = value + flip(value, axis, bit)
        bit *= 2
    return value


def pick(value, index, dim):
    half = value.shape[dim] // 2
    return lax.dynamic_slice_in_dim(value, index * half, half, dim)


def shards(
    tokens,
    cotangent,
    w_query,
    key_weight,
    value_weight,
    w_output,
    w_gate,
    w_up,
    w_down,
    gain_attn,
    gain_query,
    gain_key,
    gain_mlp,
    seq_lengths,
    seq_groups,
):
    half_rows, columns = tokens.shape
    width = columns * 2
    group_rows = half_rows * 2
    head_dim = gain_query.shape[0]
    row = lax.axis_index("row")
    col = lax.axis_index("col")
    mine, theirs = col, 1 - col
    low = jnp.bfloat16

    def exchange_tokens(local):
        own = jnp.concatenate([local, swap(local, "row")], axis=0)
        return own, swap(own, "col")

    x_own_low, x_other_low = exchange_tokens(tokens)
    gains_own = jnp.stack([gain_attn, gain_mlp])
    gains_other = swap(gains_own, "col")
    qkv_keep = jnp.concatenate(
        [pick(w_query, mine, 1), pick(key_weight, mine, 1), pick(value_weight, mine, 1)], axis=1
    )
    qkv_other = swap(
        jnp.concatenate(
            [pick(w_query, theirs, 1), pick(key_weight, theirs, 1), pick(value_weight, theirs, 1)],
            axis=1,
        ),
        "col",
    )
    mlp_keep = jnp.concatenate([pick(w_gate, mine, 1), pick(w_up, mine, 1)], axis=1)
    mlp_theirs = jnp.concatenate([pick(w_gate, theirs, 1), pick(w_up, theirs, 1)], axis=1)
    mlp_other = swap(mlp_theirs, "col")
    output_mine, output_theirs = pick(w_output, mine, 0), pick(w_output, theirs, 0)
    output_other = swap(output_theirs, "col")
    down_mine, down_theirs = pick(w_down, mine, 0), pick(w_down, theirs, 0)
    down_other = swap(down_theirs, "col")
    cot_own, cot_other = exchange_tokens(cotangent)

    segment, position = layout(seq_lengths, seq_groups, lax.axis_index("dp"), group_rows)

    def own_first(vector):
        return jnp.where(row == 0, vector, jnp.roll(vector, half_rows))

    spot = own_first(lax.iota(jnp.int32, group_rows))
    segment, position = own_first(segment), own_first(position)
    allowed = (segment[:, None] == segment[None, :]) & (spot[None, :] <= spot[:, None])

    x_own = x_own_low.astype(jnp.float32)
    query_wide = w_query.shape[1] // 2
    key_wide = key_weight.shape[1] // 2
    query_heads = query_wide // head_dim
    key_heads = key_wide // head_dim
    half = head_dim // 2
    freq = THETA ** (-(jnp.arange(half, dtype=jnp.float32) * 2.0 / head_dim))
    angle = position.astype(jnp.float32)[:, None] * freq[None, :]
    cosine, sine = jnp.cos(angle), jnp.sin(angle)
    cosine = jnp.concatenate([cosine, cosine], axis=1)
    sine = jnp.concatenate([-sine, sine], axis=1)
    allowed = allowed.astype(jnp.float32)
    turns = (gain_query[None, :], gain_key[None, :], cosine, sine, allowed)
    wide = qkv_keep.shape[1]
    normed_own, inverse_attn, sums, heads_low, attended_own = local_call(
        functools.partial(attention_kernel, query_heads, key_heads),
        [
            ((group_rows, columns), low),
            ((group_rows, 1), jnp.float32),
            ((group_rows, wide), jnp.float32),
            ((group_rows, wide), low),
            ((group_rows, query_wide), low),
        ],
        x_own_low,
        x_other_low,
        gains_own[:1],
        gains_other[:1],
        qkv_keep,
        qkv_other,
        *turns,
    )
    attended_other = swap(attended_own, "col")
    cot_flipped = flip(cot_own, "dp", 1)
    normed_halves = first_half(normed_own, "dp")

    def whole(own, other, dim):
        first = jnp.where(col == 0, own, other)
        second = jnp.where(col == 0, other, own)
        return jnp.concatenate([first, second], axis=dim)

    def both_rows(partial_value):
        arrived = swap(partial_value.astype(low), "row").astype(jnp.float32)
        return partial_value + jnp.concatenate(
            [arrived[half_rows:], arrived[:half_rows]], axis=0
        )

    attended_halves = first_half(whole(attended_own, attended_other, 1), "dp")
    partial_out = product(attended_own, output_mine) + product(attended_other, output_theirs)
    hidden = x_own + both_rows(partial_out)
    hidden_low_other = swap(hidden.astype(low), "col")
    hidden_other = hidden_low_other.astype(jnp.float32)
    act_grad = contract_cols(cot_own, down_mine) + contract_cols(cot_other, down_other)
    units = act_grad.shape[1]
    mlp_own, inverse_mlp, activated_own, grads_own = local_call(
        feed_forward_kernel,
        [
            ((group_rows, columns), low),
            ((group_rows, 1), jnp.float32),
            ((group_rows, units), low),
            ((group_rows, 2 * units), low),
        ],
        hidden,
        hidden_low_other,
        gains_own[1:],
        gains_other[1:],
        mlp_keep,
        mlp_other,
        act_grad,
    )
    mlp_halves = first_half(mlp_own, "dp")
    activated_other = swap(activated_own, "col")
    activated_halves = first_half(whole(activated_own, activated_other, 1), "dp")
    grads_other = swap(grads_own, "col")
    mlp_partial = contract_cols(grads_own, mlp_keep) + contract_cols(grads_other, mlp_theirs)
    normed_mlp_grad = both_rows(mlp_partial)
    grads_flipped = flip(grads_own, "dp", 1)
    grads_flipped_other = swap(grads_flipped, "col")
    grad_other = swap(normed_mlp_grad.astype(low), "col").astype(jnp.float32)
    scaled_own = normed_mlp_grad * gains_own[1]
    scaled_other = grad_other * gains_other[1]
    inner = (
        jnp.sum(scaled_own * hidden, axis=1) + jnp.sum(scaled_other * hidden_other, axis=1)
    )[:, None] / width
    cube = inverse_mlp**3 * inner
    hidden_grad = cot_own.astype(jnp.float32) + inverse_mlp * scaled_own - hidden * cube
    hidden_grad_other = (
        cot_other.astype(jnp.float32) + inverse_mlp * scaled_other - hidden_other * cube
    )
    gain_mlp_part = jnp.sum(
        (normed_mlp_grad * hidden * inverse_mlp)[:half_rows], axis=0
    )
    back_own = hidden_grad.astype(low)
    back_other = hidden_grad_other.astype(low)
    back_flipped = flip(back_own, "dp", 1)
    pre_own, gain_query_part, gain_key_part = local_call(
        functools.partial(attention_back_kernel, query_heads, key_heads),
        [
            ((group_rows, wide), low),
            ((1, head_dim), jnp.float32),
            ((1, head_dim), jnp.float32),
        ],
        back_own,
        back_other,
        output_mine,
        output_other,
        sums,
        heads_low,
        *turns,
    )
    pre_other = swap(pre_own, "col")

    pre_flipped = flip(pre_own, "dp", 1)
    pre_flipped_other = swap(pre_flipped, "col")
    qkv_theirs = jnp.concatenate(
        [pick(w_query, theirs, 1), pick(key_weight, theirs, 1), pick(value_weight, theirs, 1)],
        axis=1,
    )
    attn_partial = contract_cols(pre_own, qkv_keep) + contract_cols(pre_other, qkv_theirs)
    arrived = swap(attn_partial[half_rows:].astype(low), "row")
    normed_attn_grad = attn_partial[:half_rows] + arrived.astype(jnp.float32)
    x_mine = x_own[:half_rows]
    inverse_mine = inverse_attn[:half_rows]
    scaled = normed_attn_grad * gain_attn
    dot = jnp.sum(scaled * x_mine, axis=1).reshape(1, half_rows)
    dot = ((dot + swap(dot, "col")) / width).reshape(half_rows, 1)
    input_grad = (
        hidden_grad[:half_rows] + inverse_mine * scaled - x_mine * inverse_mine**3 * dot
    )
    gain_attn_part = jnp.sum(normed_attn_grad * x_mine * inverse_mine, axis=0)

    down_partial = product(activated_own, down_mine) + product(activated_other, down_theirs)
    mixed = (
        hidden[:half_rows]
        + down_partial[:half_rows]
        + swap(down_partial[half_rows:].astype(low), "row").astype(jnp.float32)
    ).astype(low)

    def woven(own, other, widths):
        first = jnp.where(col == 0, own, other)
        second = jnp.where(col == 0, other, own)
        parts, place = [], 0
        for size in widths:
            parts += [first[:, place : place + size], second[:, place : place + size]]
            place += size
        return jnp.concatenate(parts, axis=1)

    mlp_widths = (units, units)
    qkv_widths = (query_wide, key_wide, key_wide)
    mlp_total = scattered_sum(
        pair_product(
            mlp_halves,
            woven(grads_own, grads_other, mlp_widths),
            woven(grads_flipped, grads_flipped_other, mlp_widths),
        ),
        "dp",
    )
    down_total = scattered_sum(pair_product(activated_halves, cot_own, cot_flipped), "dp")
    output_total = scattered_sum(pair_product(attended_halves, back_own, back_flipped), "dp")
    qkv_total = scattered_sum(
        pair_product(
            normed_halves,
            woven(pre_own, pre_other, qkv_widths),
            woven(pre_flipped, pre_flipped_other, qkv_widths),
        ),
        "dp",
    )
    edge = 2 * query_wide
    step = 2 * key_wide

    small = jnp.concatenate([gain_attn_part, gain_mlp_part, gain_query_part[0], gain_key_part[0]])
    small = small.reshape(-1, 128)
    small = total_over(total_over(small, "dp"), "row").reshape(-1)
    heads_part = small[2 * columns :]
    heads_part = heads_part + swap(heads_part, "col")
    return (
        mixed,
        input_grad,
        qkv_total[:, :edge],
        qkv_total[:, edge : edge + step],
        qkv_total[:, edge + step :],
        output_total,
        mlp_total[:, : 2 * units],
        mlp_total[:, 2 * units :],
        down_total,
        small[:columns],
        heads_part[:head_dim],
        heads_part[head_dim:],
        small[columns : 2 * columns],
    )


def solution(mesh):
    in_specs = (
        P(("dp", "row"), "col"),
        P(("dp", "row"), "col"),
        P("col", "row"),
        P("col", "row"),
        P("col", "row"),
        P("row", "col"),
        P("col", "row"),
        P("col", "row"),
        P("row", "col"),
        P("col"),
        P(),
        P(),
        P("col"),
        P(),
        P(),
    )
    out_specs = (
        P(("dp", "row"), "col"),
        P(("dp", "row"), "col"),
        P(("col", "dp"), "row"),
        P(("col", "dp"), "row"),
        P(("col", "dp"), "row"),
        P(("row", "dp"), "col"),
        P(("col", "dp"), "row"),
        P(("col", "dp"), "row"),
        P(("row", "dp"), "col"),
        P("col"),
        P(),
        P(),
        P("col"),
    )
    return jax.shard_map(shards, mesh=mesh, in_specs=in_specs, out_specs=out_specs, check_vma=False)
```

```python
import functools
import math

import jax
import jax.numpy as jnp
from jax import lax
from jax.experimental import pallas as pl
from jax.experimental.pallas import tpu as pltpu
from jax.sharding import PartitionSpec as P

EPS = 1e-06
THETA = 1000000.0
NEGATIVE = -1e30


def layout(lengths, groups, group, slots):
    count = lengths.shape[0]
    mine = groups == group
    sizes_here = jnp.where(mine, lengths, 0)
    starts = jnp.cumsum(sizes_here) - sizes_here
    place = lax.broadcasted_iota(jnp.int32, (slots, count), 0)
    number = lax.broadcasted_iota(jnp.int32, (slots, count), 1)
    inside = mine[None, :] & (place >= starts[None, :]) & (place < (starts + sizes_here)[None, :])
    found = jnp.sum(inside.astype(jnp.int32), axis=1)
    segment = jnp.sum(jnp.where(inside, number, 0), axis=1)
    spot = lax.broadcasted_iota(jnp.int32, (slots,), 0)
    segment = jnp.where(found > 0, segment, count + spot)
    position = jnp.sum(jnp.where(inside, place - starts[None, :], 0), axis=1)
    return (segment, position)


def product(left, right):
    return jnp.dot(left, right, preferred_element_type=jnp.float32)


def contract_rows(left, right):
    return lax.dot_general(
        left, right, (((0,), (0,)), ((), ())), preferred_element_type=jnp.float32
    )


def contract_cols(left, right):
    return lax.dot_general(
        left, right, (((1,), (1,)), ((), ())), preferred_element_type=jnp.float32
    )


VMEM_BYTES = 44 * 1024 * 1024


def local_call(body, shapes, *operands):
    return pl.pallas_call(
        body,
        out_shape=[jax.ShapeDtypeStruct(shape, dtype) for shape, dtype in shapes],
        in_specs=[pl.BlockSpec(memory_space=pltpu.VMEM)] * len(operands),
        out_specs=[pl.BlockSpec(memory_space=pltpu.VMEM)] * len(shapes),
        compiler_params=pltpu.CompilerParams(vmem_limit_bytes=VMEM_BYTES),
    )(*operands)


def half_turn(value_rows):
    return pltpu.roll(value_rows, value_rows.shape[1] // 2, 1)


def head_scale(value_rows):
    return lax.rsqrt(jnp.mean(value_rows * value_rows, axis=1, keepdims=True) + EPS)


def head_cols(index, size):
    return slice(index * size, (index + 1) * size)


def softmax_rows(query, key, allowed, scale):
    scores = jnp.where(allowed, contract_cols(query, key) * scale, NEGATIVE)
    exponent = jnp.exp(scores - jnp.max(scores, axis=1, keepdims=True))
    return exponent / jnp.sum(exponent, axis=1, keepdims=True)


def attention_kernel(
    query_heads,
    key_heads,
    x_own_ref,
    x_other_ref,
    gain_own_ref,
    gain_other_ref,
    keep_ref,
    other_ref,
    gain_query_ref,
    gain_key_ref,
    cosine_ref,
    sine_ref,
    allowed_ref,
    normed_ref,
    inverse_ref,
    sums_ref,
    low_ref,
    attended_ref,
):
    size = gain_query_ref.shape[1]
    scale = 1.0 / math.sqrt(size)
    own = x_own_ref[...].astype(jnp.float32)
    other = x_other_ref[...].astype(jnp.float32)
    total = jnp.sum(own * own, axis=1, keepdims=True) + jnp.sum(
        other * other, axis=1, keepdims=True
    )
    inverse = lax.rsqrt(total / (2 * own.shape[1]) + EPS)
    inverse_ref[...] = inverse
    normed = (own * inverse * gain_own_ref[...]).astype(jnp.bfloat16)
    normed_ref[...] = normed
    normed_other = (other * inverse * gain_other_ref[...]).astype(jnp.bfloat16)
    sums_ref[...] = product(normed, keep_ref[...]) + product(normed_other, other_ref[...])
    cosine, sine = cosine_ref[...], sine_ref[...]
    for head in range(query_heads + key_heads):
        cols = head_cols(head, size)
        gain = gain_query_ref[...] if head < query_heads else gain_key_ref[...]
        one = sums_ref[:, cols]
        one = one * head_scale(one) * gain
        low_ref[:, cols] = (one * cosine + half_turn(one) * sine).astype(jnp.bfloat16)
    values = slice((query_heads + key_heads) * size, (query_heads + 2 * key_heads) * size)
    low_ref[:, values] = sums_ref[:, values].astype(jnp.bfloat16)
    allowed = allowed_ref[...] > 0.0
    share = query_heads // key_heads
    for head in range(query_heads):
        key = low_ref[:, head_cols(query_heads + head // share, size)]
        value = low_ref[:, head_cols(query_heads + key_heads + head // share, size)]
        cols = head_cols(head, size)
        probs = softmax_rows(low_ref[:, cols], key, allowed, scale)
        attended_ref[:, cols] = product(probs.astype(jnp.bfloat16), value).astype(jnp.bfloat16)


def attention_back_kernel(
    query_heads,
    key_heads,
    back_own_ref,
    back_other_ref,
    output_own_ref,
    output_other_ref,
    sums_ref,
    low_ref,
    gain_query_ref,
    gain_key_ref,
    cosine_ref,
    sine_ref,
    allowed_ref,
    pre_ref,
    gain_query_grad_ref,
    gain_key_grad_ref,
):
    size = gain_query_ref.shape[1]
    scale = 1.0 / math.sqrt(size)
    grad = (
        contract_cols(back_own_ref[...], output_own_ref[...])
        + contract_cols(back_other_ref[...], output_other_ref[...])
    ).astype(jnp.bfloat16)
    cosine, sine = cosine_ref[...], sine_ref[...]
    allowed = allowed_ref[...] > 0.0
    share = query_heads // key_heads

    def pull(rotated, head, gain):
        cols = head_cols(head, size)
        turned = rotated * cosine - half_turn(rotated) * sine
        one = sums_ref[:, cols]
        ratio = head_scale(one)
        weighted = turned * gain
        mean = jnp.mean(weighted * one, axis=1, keepdims=True)
        pre_ref[:, cols] = (ratio * weighted - one * ratio**3 * mean).astype(jnp.bfloat16)
        return jnp.sum(turned * one * ratio, axis=0, keepdims=True)

    gain_query_grad = jnp.zeros((1, size), jnp.float32)
    gain_key_grad = jnp.zeros((1, size), jnp.float32)
    for pair in range(key_heads):
        key = low_ref[:, head_cols(query_heads + pair, size)]
        value = low_ref[:, head_cols(query_heads + key_heads + pair, size)]
        key_rotated = jnp.zeros((key.shape[0], size), jnp.float32)
        value_grad = jnp.zeros((key.shape[0], size), jnp.float32)
        for head in range(pair * share, (pair + 1) * share):
            query = low_ref[:, head_cols(head, size)]
            grad_head = grad[:, head_cols(head, size)]
            probs = softmax_rows(query, key, allowed, scale)
            prob_grad = contract_cols(grad_head, value)
            inner = jnp.sum(probs * prob_grad, axis=1, keepdims=True)
            score_grad = (probs * (prob_grad - inner)).astype(jnp.bfloat16)
            gain_query_grad += pull(product(score_grad, key) * scale, head, gain_query_ref[...])
            key_rotated += contract_rows(score_grad, query)
            value_grad += contract_rows(probs.astype(jnp.bfloat16), grad_head)
        gain_key_grad += pull(key_rotated * scale, query_heads + pair, gain_key_ref[...])
        pre_ref[:, head_cols(query_heads + key_heads + pair, size)] = value_grad.astype(
            jnp.bfloat16
        )
    gain_query_grad_ref[...] = gain_query_grad
    gain_key_grad_ref[...] = gain_key_grad


def feed_forward_kernel(
    hidden_ref,
    other_ref,
    gain_own_ref,
    gain_other_ref,
    keep_ref,
    swapped_ref,
    act_grad_ref,
    normed_ref,
    inverse_ref,
    activated_ref,
    grads_ref,
):
    hidden = hidden_ref[...]
    other = other_ref[...].astype(jnp.float32)
    total = jnp.sum(hidden * hidden, axis=1, keepdims=True) + jnp.sum(
        other * other, axis=1, keepdims=True
    )
    inverse = lax.rsqrt(total / (2 * hidden.shape[1]) + EPS)
    inverse_ref[...] = inverse
    normed = (hidden * inverse * gain_own_ref[...]).astype(jnp.bfloat16)
    normed_ref[...] = normed
    normed_other = (other * inverse * gain_other_ref[...]).astype(jnp.bfloat16)
    units = activated_ref.shape[1]
    step = 256
    for start in range(0, units, step):
        low, high = slice(start, start + step), slice(units + start, units + start + step)
        gate = product(normed, keep_ref[:, low]) + product(normed_other, swapped_ref[:, low])
        up = product(normed, keep_ref[:, high]) + product(normed_other, swapped_ref[:, high])
        sigmoid = jax.nn.sigmoid(gate)
        silu = gate * sigmoid
        activated_ref[:, low] = (silu * up).astype(jnp.bfloat16)
        act_grad = act_grad_ref[:, low]
        grads_ref[:, low] = (act_grad * up * sigmoid * (1.0 + gate * (1.0 - sigmoid))).astype(
            jnp.bfloat16
        )
        grads_ref[:, high] = (act_grad * silu).astype(jnp.bfloat16)


def swap(value, axis):
    return lax.ppermute(value, axis, [(0, 1), (1, 0)])


def flip(value, axis, bit):
    size = lax.axis_size(axis)
    return lax.ppermute(value, axis, [(i, i ^ bit) for i in range(size)])


def relative_order(size):
    bits = size.bit_length() - 1
    return [int(format(k, "b").zfill(bits)[::-1], 2) if bits else 0 for k in range(size)]


def relative_blocks(value_rows, axis):
    size = lax.axis_size(axis)
    me = lax.axis_index(axis)
    width = value_rows.shape[1] // size
    turned = value_rows.T.reshape(size, width, value_rows.shape[0])
    parts = [
        lax.dynamic_index_in_dim(turned, me ^ j, 0, keepdims=False) for j in relative_order(size)
    ]
    return jnp.concatenate(parts, axis=0)


def first_half(left, axis):
    blocks = relative_blocks(left, axis)
    half = blocks.shape[0] // 2
    return blocks[:half], flip(blocks[half:], axis, 1)


def after(value, anchor):
    return lax.optimization_barrier((value, anchor))[0]


def split_half(kept):
    half = kept.shape[0] // 2
    return kept[:half], kept[half:].astype(jnp.bfloat16)


def scattered_sum(kept, away, axis, anchors):
    first = kept
    bit = 2
    size = lax.axis_size(axis)
    while bit < size:
        arrived = flip(away, axis, bit)
        arrived = after(arrived, anchors[0 if bit == 2 else 1])
        kept = kept + arrived.astype(jnp.float32)
        first = kept if bit == 2 else first
        bit *= 2
        if bit < size:
            kept, away = split_half(kept)
    return kept, first


def pair_product(halves, right, right_arrived):
    return product(halves[0], right) + product(halves[1], right_arrived)


def total_over(value, axis, bit=1):
    while bit < lax.axis_size(axis):
        value = value + flip(value, axis, bit)
        bit *= 2
    return value


def pick(value, index, dim):
    half = value.shape[dim] // 2
    return lax.dynamic_slice_in_dim(value, index * half, half, dim)


def shards(
    tokens,
    cotangent,
    w_query,
    key_weight,
    value_weight,
    w_output,
    w_gate,
    w_up,
    w_down,
    gain_attn,
    gain_query,
    gain_key,
    gain_mlp,
    seq_lengths,
    seq_groups,
):
    half_rows, columns = tokens.shape
    width = columns * 2
    group_rows = half_rows * 2
    head_dim = gain_query.shape[0]
    row = lax.axis_index("row")
    col = lax.axis_index("col")
    mine, theirs = col, 1 - col
    low = jnp.bfloat16

    def exchange_tokens(local):
        own = jnp.concatenate([local, swap(local, "row")], axis=0)
        return own, swap(own, "col")

    x_own_low, x_other_low = exchange_tokens(tokens)
    gains_own = jnp.stack([gain_attn, gain_mlp])
    gains_other = swap(gains_own, "col")
    qkv_keep = jnp.concatenate(
        [pick(w_query, mine, 1), pick(key_weight, mine, 1), pick(value_weight, mine, 1)], axis=1
    )
    qkv_other = swap(
        jnp.concatenate(
            [pick(w_query, theirs, 1), pick(key_weight, theirs, 1), pick(value_weight, theirs, 1)],
            axis=1,
        ),
        "col",
    )
    mlp_keep = jnp.concatenate([pick(w_gate, mine, 1), pick(w_up, mine, 1)], axis=1)
    mlp_theirs = jnp.concatenate([pick(w_gate, theirs, 1), pick(w_up, theirs, 1)], axis=1)
    mlp_other = swap(mlp_theirs, "col")
    output_mine, output_theirs = pick(w_output, mine, 0), pick(w_output, theirs, 0)
    output_other = swap(output_theirs, "col")
    down_mine, down_theirs = pick(w_down, mine, 0), pick(w_down, theirs, 0)
    down_other = swap(down_theirs, "col")
    cot_own, cot_other = exchange_tokens(cotangent)

    segment, position = layout(seq_lengths, seq_groups, lax.axis_index("dp"), group_rows)

    def own_first(vector):
        return jnp.where(row == 0, vector, jnp.roll(vector, half_rows))

    spot = own_first(lax.iota(jnp.int32, group_rows))
    segment, position = own_first(segment), own_first(position)
    allowed = (segment[:, None] == segment[None, :]) & (spot[None, :] <= spot[:, None])

    x_own = x_own_low.astype(jnp.float32)
    query_wide = w_query.shape[1] // 2
    key_wide = key_weight.shape[1] // 2
    query_heads = query_wide // head_dim
    key_heads = key_wide // head_dim
    half = head_dim // 2
    freq = THETA ** (-(jnp.arange(half, dtype=jnp.float32) * 2.0 / head_dim))
    angle = position.astype(jnp.float32)[:, None] * freq[None, :]
    cosine, sine = jnp.cos(angle), jnp.sin(angle)
    cosine = jnp.concatenate([cosine, cosine], axis=1)
    sine = jnp.concatenate([-sine, sine], axis=1)
    allowed = allowed.astype(jnp.float32)
    turns = (gain_query[None, :], gain_key[None, :], cosine, sine, allowed)
    wide = qkv_keep.shape[1]
    normed_own, inverse_attn, sums, heads_low, attended_own = local_call(
        functools.partial(attention_kernel, query_heads, key_heads),
        [
            ((group_rows, columns), low),
            ((group_rows, 1), jnp.float32),
            ((group_rows, wide), jnp.float32),
            ((group_rows, wide), low),
            ((group_rows, query_wide), low),
        ],
        x_own_low,
        x_other_low,
        gains_own[:1],
        gains_other[:1],
        qkv_keep,
        qkv_other,
        *turns,
    )
    attended_other = swap(attended_own, "col")
    cot_flipped = flip(cot_own, "dp", 1)
    normed_halves = first_half(normed_own, "dp")

    def whole(own, other, dim):
        first = jnp.where(col == 0, own, other)
        second = jnp.where(col == 0, other, own)
        return jnp.concatenate([first, second], axis=dim)

    def both_rows(partial_value):
        arrived = swap(partial_value.astype(low), "row").astype(jnp.float32)
        return partial_value + jnp.concatenate(
            [arrived[half_rows:], arrived[:half_rows]], axis=0
        )

    attended_halves = first_half(whole(attended_own, attended_other, 1), "dp")
    partial_out = product(attended_own, output_mine) + product(attended_other, output_theirs)
    hidden = x_own + both_rows(partial_out)
    hidden_low_other = swap(hidden.astype(low), "col")
    hidden_other = hidden_low_other.astype(jnp.float32)
    act_grad = contract_cols(cot_own, down_mine) + contract_cols(cot_other, down_other)
    units = act_grad.shape[1]
    mlp_own, inverse_mlp, activated_own, grads_own = local_call(
        feed_forward_kernel,
        [
            ((group_rows, columns), low),
            ((group_rows, 1), jnp.float32),
            ((group_rows, units), low),
            ((group_rows, 2 * units), low),
        ],
        hidden,
        hidden_low_other,
        gains_own[1:],
        gains_other[1:],
        mlp_keep,
        mlp_other,
        act_grad,
    )
    mlp_halves = first_half(mlp_own, "dp")
    activated_other = swap(activated_own, "col")
    activated_halves = first_half(whole(activated_own, activated_other, 1), "dp")
    grads_other = swap(grads_own, "col")
    mlp_partial = contract_cols(grads_own, mlp_keep) + contract_cols(grads_other, mlp_theirs)
    normed_mlp_grad = both_rows(mlp_partial)
    down_sides = (activated_halves[0], after(activated_halves[1], normed_mlp_grad))
    down_halves = split_half(pair_product(down_sides, cot_own, cot_flipped))
    grads_flipped = flip(grads_own, "dp", 1)
    grads_flipped_other = swap(grads_flipped, "col")
    grad_other = swap(normed_mlp_grad.astype(low), "col").astype(jnp.float32)
    scaled_own = normed_mlp_grad * gains_own[1]
    scaled_other = grad_other * gains_other[1]
    inner = (
        jnp.sum(scaled_own * hidden, axis=1) + jnp.sum(scaled_other * hidden_other, axis=1)
    )[:, None] / width
    cube = inverse_mlp**3 * inner
    hidden_grad = cot_own.astype(jnp.float32) + inverse_mlp * scaled_own - hidden * cube
    hidden_grad_other = (
        cot_other.astype(jnp.float32) + inverse_mlp * scaled_other - hidden_other * cube
    )
    gain_mlp_part = jnp.sum(
        (normed_mlp_grad * hidden * inverse_mlp)[:half_rows], axis=0
    )
    back_own = hidden_grad.astype(low)
    back_other = hidden_grad_other.astype(low)
    qkv_widths = (query_wide, key_wide, key_wide)
    mlp_widths = (units, units)
    def woven(own, other, widths):
        first = jnp.where(col == 0, own, other)
        second = jnp.where(col == 0, other, own)
        parts, place = [], 0
        for size in widths:
            parts += [first[:, place : place + size], second[:, place : place + size]]
            place += size
        return jnp.concatenate(parts, axis=1)

    mlp_product = split_half(
        pair_product(
            mlp_halves,
            woven(grads_own, grads_other, mlp_widths),
            woven(grads_flipped, grads_flipped_other, mlp_widths),
        )
    )
    back_flipped = flip(back_own, "dp", 1)
    pre_own, gain_query_part, gain_key_part = local_call(
        functools.partial(attention_back_kernel, query_heads, key_heads),
        [
            ((group_rows, wide), low),
            ((1, head_dim), jnp.float32),
            ((1, head_dim), jnp.float32),
        ],
        after(back_own, (mlp_product[1], down_halves[1])),
        back_other,
        output_mine,
        output_other,
        sums,
        heads_low,
        *turns,
    )
    pre_other = swap(pre_own, "col")

    pre_flipped = flip(pre_own, "dp", 1)
    pre_flipped_other = swap(pre_flipped, "col")
    qkv_theirs = jnp.concatenate(
        [pick(w_query, theirs, 1), pick(key_weight, theirs, 1), pick(value_weight, theirs, 1)],
        axis=1,
    )
    attn_partial = contract_cols(pre_own, qkv_keep) + contract_cols(pre_other, qkv_theirs)
    arrived = swap(attn_partial[half_rows:].astype(low), "row")
    normed_attn_grad = attn_partial[:half_rows] + arrived.astype(jnp.float32)
    x_mine = x_own[:half_rows]
    inverse_mine = inverse_attn[:half_rows]
    scaled = normed_attn_grad * gain_attn
    dot = jnp.sum(scaled * x_mine, axis=1).reshape(1, half_rows)
    dot = ((dot + swap(dot, "col")) / width).reshape(half_rows, 1)
    input_grad = (
        hidden_grad[:half_rows] + inverse_mine * scaled - x_mine * inverse_mine**3 * dot
    )
    gain_attn_part = jnp.sum(normed_attn_grad * x_mine * inverse_mine, axis=0)

    down_partial = product(activated_own, down_mine) + product(activated_other, down_theirs)
    mixed = (
        hidden[:half_rows]
        + down_partial[:half_rows]
        + swap(down_partial[half_rows:].astype(low), "row").astype(jnp.float32)
    ).astype(low)

    down_total, _ = scattered_sum(*down_halves, "dp", (pre_own, input_grad))
    mlp_total, _ = scattered_sum(*mlp_product, "dp", (attn_partial, input_grad))
    output_halves = split_half(
        pair_product(attended_halves, back_own, after(back_flipped, pre_own))
    )
    output_total, _ = scattered_sum(*output_halves, "dp", (input_grad, input_grad))
    qkv_product = split_half(
        pair_product(
            normed_halves,
            woven(pre_own, pre_other, qkv_widths),
            woven(pre_flipped, pre_flipped_other, qkv_widths),
        )
    )
    qkv_total, qkv_first = scattered_sum(*qkv_product, "dp", (input_grad, input_grad))
    edge = 2 * query_wide
    step = 2 * key_wide

    small = jnp.concatenate([gain_attn_part, gain_mlp_part, gain_query_part[0], gain_key_part[0]])
    small = total_over(small.reshape(-1, 128), "row")
    small = after(small + flip(small, "dp", 1), qkv_first)
    small = total_over(small, "dp", 2).reshape(-1)
    heads_part = small[2 * columns :]
    heads_part = heads_part + swap(heads_part, "col")
    return (
        mixed,
        input_grad,
        qkv_total[:, :edge],
        qkv_total[:, edge : edge + step],
        qkv_total[:, edge + step :],
        output_total,
        mlp_total[:, : 2 * units],
        mlp_total[:, 2 * units :],
        down_total,
        small[:columns],
        heads_part[:head_dim],
        heads_part[head_dim:],
        small[columns : 2 * columns],
    )


def solution(mesh):
    in_specs = (
        P(("dp", "row"), "col"),
        P(("dp", "row"), "col"),
        P("col", "row"),
        P("col", "row"),
        P("col", "row"),
        P("row", "col"),
        P("col", "row"),
        P("col", "row"),
        P("row", "col"),
        P("col"),
        P(),
        P(),
        P("col"),
        P(),
        P(),
    )
    out_specs = (
        P(("dp", "row"), "col"),
        P(("dp", "row"), "col"),
        P(("col", "dp"), "row"),
        P(("col", "dp"), "row"),
        P(("col", "dp"), "row"),
        P(("row", "dp"), "col"),
        P(("col", "dp"), "row"),
        P(("col", "dp"), "row"),
        P(("row", "dp"), "col"),
        P("col"),
        P(),
        P(),
        P("col"),
    )
    return jax.shard_map(shards, mesh=mesh, in_specs=in_specs, out_specs=out_specs, check_vma=False)
```
